256 devices in a mesh: tm: 8 (over x_hi, y), row: 32 (over x_lo, z, core).
Axes of the slice: x: 4 (x_hi: 2, x_lo: 2; x = x_hi * 2 + x_lo), y: 4, z: 8, core: 2. Of those that a mesh axis runs over, the one named last changes fastest.
Arguments:
- voltage: bfloat16 [128, 128, 128, 512], P('tm', 'row'), may hold values from -6 to 6
Outputs:
- beam_power: float32 [8, 256, 128, 128], P('tm', 'row')
The draws below stay inside these ranges and needn't reach their ends.
All inputs are finite; a program needn't handle non-finite values.
Results may differ from the reference program's by a relative error of at most 0.0041.
Values may be sent and summed in bfloat16 or wider, within the bound.
A program may use at most 128 MiB of HBM per device.

```python
import math
import jax
import jax.numpy as jnp
from jax import lax

R = 128
C = 128
NCH = 256
TAPS = 4
FR = 16
FRAMES = 128


def block_scale(key, dims, split, smallest, high):
    gain = 1.0
    for dim, blocks in split:
        heights = jax.random.uniform(jax.random.fold_in(jax.random.fold_in(key, 6), dim), (blocks,), jnp.float32, smallest / len(split), high / len(split))
        gain = gain * jnp.repeat(jnp.exp(heights), dims[dim] // blocks).reshape((-1,) + (1,) * (len(dims) - 1 - dim))
    return gain


def gaussian(stream_key, extent, scale, reach, pieces=(), kind=jnp.bfloat16):
    array = scale * jax.random.normal(stream_key, extent, jnp.float32)
    if pieces:
        array = array * block_scale(stream_key, extent, pieces, -0.22, 0.18)
    return jnp.clip(array, -reach, reach).astype(kind)


def setup_inputs(seed: int = 0) -> dict:
    key_of = jax.random.split(jax.random.key(seed), 2)
    voltage = gaussian(key_of[0], (FRAMES, R, C, 2 * NCH), 1.0, 6.0, ((0, 8), (1, 32)))
    return {"voltage": voltage}


def pfb_window(taps, channels):
    points = jnp.arange(taps * channels, dtype=jnp.float32)
    offset = (points + 0.5) / channels - taps / 2.0
    taper = 0.5 - 0.5 * jnp.cos(2.0 * math.pi * (points + 0.5) / (taps * channels))
    shaped = (jnp.sinc(offset) * taper).reshape(taps, channels)
    return jnp.concatenate([shaped, shaped], axis=1)

def dft_table(length):
    indices = jnp.arange(length, dtype=jnp.int32)
    products = indices[:, None] * indices[None, :] % length
    phase_angle = products.astype(jnp.float32) * (2.0 * math.pi / length)
    norm_scale = 1.0 / math.sqrt(length)
    cosine = jnp.cos(phase_angle) * norm_scale
    sine = jnp.sin(phase_angle) * norm_scale
    upper = jnp.stack([cosine, -sine], axis=1)
    bottom = jnp.stack([sine, cosine], axis=1)
    return jnp.stack([upper, bottom], axis=0).astype(jnp.bfloat16)

def reference(voltage):
    frames_total = voltage.shape[0]
    weights = pfb_window(TAPS, NCH)
    fine_table = dft_table(NCH).reshape(2 * NCH, 2 * NCH)
    column_table = dft_table(C).astype(jnp.float32)
    row_table = dft_table(R).astype(jnp.float32)

    def one_frame(frame_index):
        summed = jnp.zeros((R, C, 2 * NCH), jnp.float32)
        for tap_index in range(TAPS):
            source = (frame_index - (TAPS - 1) + tap_index + frames_total) % frames_total
            picked = lax.dynamic_index_in_dim(voltage, source.astype(jnp.int32), 0, keepdims=False)
            summed = summed + weights[tap_index] * picked.astype(jnp.float32)
        weighted = summed.astype(jnp.bfloat16)
        spectrum = jnp.dot(weighted.reshape(R * C, 2 * NCH), fine_table, preferred_element_type=jnp.float32)
        spectrum = lax.optimization_barrier(spectrum.astype(jnp.bfloat16)).reshape(R, C, 2, NCH)
        column_beam = jnp.einsum('rcpk,pcqv->rqkv', spectrum.astype(jnp.float32), column_table)
        column_beam = lax.optimization_barrier(column_beam.astype(jnp.bfloat16))
        beam_field = jnp.einsum('rqkv,qrsu->skuv', column_beam.astype(jnp.float32), row_table)
        return lax.optimization_barrier(jnp.sum(beam_field * beam_field, axis=0))

    def one_slab(slab_index):

        def advance(total, offset):
            return (total + one_frame(slab_index * FR + offset), None)
        total, unused = lax.scan(advance, jnp.zeros((NCH, R, C), jnp.float32), jnp.arange(FR, dtype=jnp.int32))
        return total / FR
    return lax.map(one_slab, jnp.arange(frames_total // FR, dtype=jnp.int32))
```

```python
import math

import jax
import jax.numpy as jnp
import ml_dtypes
import numpy as np
from jax import lax
from jax.experimental import pallas as pl
from jax.experimental.pallas import tpu as pltpu
from jax.sharding import PartitionSpec as P

TAPS = 4
HISTORY = TAPS - 1
NCH = 256
C = 128
R = 128
FR = 16
NROW = 32
NTM = 8
RHERE = R // NROW
KHERE = NCH // NROW
RK = RHERE * KHERE
MESH_ID = pl.DeviceIdType.MESH


def pfb_window():
    points = np.arange(TAPS * NCH, dtype=np.float64)
    offset = (points + 0.5) / NCH - TAPS / 2.0
    taper = 0.5 - 0.5 * np.cos(2.0 * math.pi * (points + 0.5) / (TAPS * NCH))
    shaped = (np.sinc(offset) * taper).reshape(TAPS, NCH)
    return np.concatenate([shaped, shaped], axis=1).astype(np.float32)


def dft_table(length):
    indices = np.arange(length)
    angle = (indices[:, None] * indices[None, :] % length) * (2.0 * math.pi / length)
    cosine = np.cos(angle) / math.sqrt(length)
    sine = np.sin(angle) / math.sqrt(length)
    upper = np.stack([cosine, -sine], axis=1)
    bottom = np.stack([sine, cosine], axis=1)
    return np.stack([upper, bottom], axis=0).astype(np.float32).astype(ml_dtypes.bfloat16)


def tables():
    fine = dft_table(NCH).reshape(2 * NCH, 2, NROW, KHERE).transpose(2, 1, 3, 0)
    fine = fine.reshape(2 * NCH, 2 * NCH)
    column = dft_table(C).reshape(2 * C, 2 * C)
    row = dft_table(R).transpose(2, 3, 0, 1).reshape(2 * R, 2 * R)
    return fine, column, row


def kernel(
    volt_hbm, w_hbm, fine_hbm, col_hbm, row_hbm, out_hbm,
    volt, w, fine, col, row, weighted, send, recv, mid, acc,
    load_sem, table_sem, halo_sem, send_sem, recv_sem, out_sem,
):
    tm = lax.axis_index("tm")
    me = lax.axis_index("row")
    x, z, core = me // 16, (me // 2) % 8, me % 2
    after, before = (tm + 1) % NTM, (tm + NTM - 1) % NTM

    def partner(e):
        dz = (3 * (e // 4 + 1)) % 8
        dx = 1 - (e // 2) % 2
        dc = 1 - e % 2
        return (((x + dx) % 2) * 8 + (z + dz) % 8) * 2 + (core + dc) % 2

    barrier = pltpu.get_barrier_semaphore()

    def greet(e, carry):
        pl.semaphore_signal(barrier, inc=1, device_id={"row": partner(e)}, device_id_type=MESH_ID)
        return carry

    lax.fori_loop(0, NROW - 1, greet, 0)
    for neighbour in (before, after):
        pl.semaphore_signal(barrier, inc=1, device_id={"tm": neighbour}, device_id_type=MESH_ID)

    def load(g):
        return pltpu.make_async_copy(volt_hbm.at[g], volt.at[g + HISTORY], load_sem.at[g])

    table_copies = [
        pltpu.make_async_copy(a, b, table_sem.at[i])
        for i, (a, b) in enumerate(
            ((w_hbm, w), (fine_hbm, fine), (col_hbm, col), (row_hbm, row))
        )
    ]
    table_copies[0].start()
    for g in range(TAPS):
        load(g).start()
    for copy in table_copies[1:]:
        copy.start()

    def load_more(g, carry):
        load(g).start()
        return carry

    lax.fori_loop(TAPS, FR, load_more, 0)

    halo = pltpu.make_async_remote_copy(
        src_ref=volt_hbm.at[pl.ds(FR - HISTORY, HISTORY)],
        dst_ref=volt.at[pl.ds(0, HISTORY)],
        send_sem=halo_sem.at[0],
        recv_sem=halo_sem.at[1],
        device_id={"tm": after},
        device_id_type=MESH_ID,
    )

    def spectrum(g):
        def chunk(i, carry):
            rows = pl.ds(pl.multiple_of(i * 16, 16), 16)
            total = w[0:1, :] * volt[g, rows, :].astype(jnp.float32)
            for tap in range(1, TAPS):
                total = total + w[tap : tap + 1, :] * volt[g + tap, rows, :].astype(jnp.float32)
            weighted[rows, :] = total.astype(jnp.bfloat16)
            return carry

        lax.fori_loop(0, RHERE * C // 16, chunk, 0, unroll=2)
        for pair in range(RHERE // 2):
            out = lax.dot_general(
                fine[...],
                weighted[pair * 2 * C : (pair + 1) * 2 * C, :],
                (((1,), (1,)), ((), ())),
                preferred_element_type=jnp.float32,
            ).reshape(NROW, 2, KHERE, 2 * C)
            for q in range(2):
                both = jnp.concatenate([out[:, q, :, :C], out[:, q, :, C:]], axis=1)
                send[g, :, pair * 2 * KHERE : (pair + 1) * 2 * KHERE, q * C : (q + 1) * C] = (
                    both.astype(jnp.bfloat16)
                )

    def dispatch(g):
        def one(e, carry):
            to = partner(e)
            pltpu.make_async_remote_copy(
                src_ref=send.at[g, to],
                dst_ref=recv.at[g, me],
                send_sem=send_sem.at[g],
                recv_sem=recv_sem.at[g],
                device_id={"row": to},
                device_id_type=MESH_ID,
            ).start()
            return carry

        lax.fori_loop(0, NROW - 1, one, 0)
        pltpu.make_async_copy(send.at[g, me], recv.at[g, me], recv_sem.at[g]).start()

    def beams(g):
        pltpu.make_async_copy(send.at[g], recv.at[g], recv_sem.at[g]).wait()
        for part in range(4):
            rows = R * KHERE // 4
            block = recv[g, pl.ds(part * NROW // 4, NROW // 4)].reshape(rows, 2 * C)
            out = jnp.dot(block, col[...], preferred_element_type=jnp.float32)
            for q in range(2):
                mid[q, part * rows : (part + 1) * rows, :] = out[:, q * C : (q + 1) * C]
        for pair in range(KHERE // 2):
            sides = []
            for k in (2 * pair, 2 * pair + 1):
                parts = [mid[q, pl.ds(k, R, stride=KHERE), :] for q in range(2)]
                sides.append(jnp.concatenate(parts, axis=0).astype(jnp.bfloat16))
            field = jnp.dot(
                row[...], jnp.concatenate(sides, axis=1), preferred_element_type=jnp.float32
            )
            power = field[:R] * field[:R] + field[R:] * field[R:]
            for i in range(2):
                acc[2 * pair + i] += power[:, i * C : (i + 1) * C]

    table_copies[0].wait()
    for g in range(TAPS):
        load(g).wait()
    table_copies[1].wait()
    spectrum(HISTORY)
    pl.semaphore_wait(barrier, NROW - 1 + 2)
    dispatch(HISTORY)
    halo.start()

    def ahead(g, carry):
        load(g).wait()
        spectrum(g)
        dispatch(g)
        return carry

    lax.fori_loop(TAPS, FR, ahead, 0)
    halo.wait()

    def first(g, carry):
        spectrum(g)
        dispatch(g)
        return carry

    lax.fori_loop(0, HISTORY, first, 0)

    acc[...] = jnp.zeros_like(acc)
    table_copies[2].wait()
    table_copies[3].wait()

    def gather(i, carry):
        beams((i + HISTORY) % FR)
        return carry

    lax.fori_loop(0, FR, gather, 0)
    acc[...] = acc[...] * (1.0 / FR)
    result = pltpu.make_async_copy(acc, out_hbm, out_sem.at[0])
    result.start()

    def sent(g, carry):
        some = pl.ds(0, NROW - 1)
        pltpu.make_async_copy(send.at[g, some], recv.at[g, some], send_sem.at[g]).wait()
        return carry

    lax.fori_loop(0, FR, sent, 0)
    result.wait()


def body(voltage):
    frames, rows, columns, width = voltage.shape
    any_space = pl.BlockSpec(memory_space=pl.ANY)
    fine, column, row = tables()
    power = pl.pallas_call(
        kernel,
        out_shape=jax.ShapeDtypeStruct((KHERE, R, C), jnp.float32),
        in_specs=[any_space] * 5,
        out_specs=any_space,
        scratch_shapes=[
            pltpu.VMEM((FR + HISTORY, RHERE * C, 2 * NCH), jnp.bfloat16),
            pltpu.VMEM((TAPS, 2 * NCH), jnp.float32),
            pltpu.VMEM((2 * NCH, 2 * NCH), jnp.bfloat16),
            pltpu.VMEM((2 * C, 2 * C), jnp.bfloat16),
            pltpu.VMEM((2 * R, 2 * R), jnp.bfloat16),
            pltpu.VMEM((RHERE * C, 2 * NCH), jnp.bfloat16),
            pltpu.VMEM((FR, NROW, RK, 2 * C), jnp.bfloat16),
            pltpu.VMEM((FR, NROW, RK, 2 * C), jnp.bfloat16),
            pltpu.VMEM((2, R * KHERE, C), jnp.float32),
            pltpu.VMEM((KHERE, R, C), jnp.float32),
            pltpu.SemaphoreType.DMA((FR,)),
            pltpu.SemaphoreType.DMA((4,)),
            pltpu.SemaphoreType.DMA((2,)),
            pltpu.SemaphoreType.DMA((FR,)),
            pltpu.SemaphoreType.DMA((FR,)),
            pltpu.SemaphoreType.DMA((1,)),
        ],
        compiler_params=pltpu.CompilerParams(
            collective_id=0, has_side_effects=True, vmem_limit_bytes=48 * 1024 * 1024
        ),
        name="beamformer",
    )(
        voltage.reshape(frames, rows * columns, width),
        jnp.asarray(pfb_window()),
        jnp.asarray(fine),
        jnp.asarray(column),
        jnp.asarray(row),
    )
    return power[None]


def solution(mesh):
    return jax.shard_map(
        body,
        mesh=mesh,
        in_specs=(P("tm", "row", None, None),),
        out_specs=P("tm", "row", None, None),
        check_vma=False,
    )
```

```python
import math

import jax
import jax.numpy as jnp
import ml_dtypes
import numpy as np
from jax import lax
from jax.experimental import pallas as pl
from jax.experimental.pallas import tpu as pltpu
from jax.sharding import PartitionSpec as P

TAPS = 4
HISTORY = TAPS - 1
NCH = 256
C = 128
R = 128
FR = 16
NROW = 32
NTM = 8
RHERE = R // NROW
KHERE = NCH // NROW
RK = RHERE * KHERE
VMEM_BYTES = 54656 * 1024
MESH_ID = pl.DeviceIdType.MESH


def pfb_window():
    points = np.arange(TAPS * NCH, dtype=np.float64)
    offset = (points + 0.5) / NCH - TAPS / 2.0
    taper = 0.5 - 0.5 * np.cos(2.0 * math.pi * (points + 0.5) / (TAPS * NCH))
    shaped = (np.sinc(offset) * taper).reshape(TAPS, NCH)
    return np.concatenate([shaped, shaped], axis=1).astype(np.float32)


def dft_table(length):
    indices = np.arange(length)
    angle = (indices[:, None] * indices[None, :] % length) * (2.0 * math.pi / length)
    cosine = np.cos(angle) / math.sqrt(length)
    sine = np.sin(angle) / math.sqrt(length)
    upper = np.stack([cosine, -sine], axis=1)
    bottom = np.stack([sine, cosine], axis=1)
    return np.stack([upper, bottom], axis=0).astype(np.float32).astype(ml_dtypes.bfloat16)


def tables():
    fine = dft_table(NCH).reshape(2 * NCH, 2, NROW, KHERE).transpose(2, 1, 3, 0)
    fine = fine.reshape(2 * NCH, 2 * NCH)
    column = dft_table(C).reshape(2 * C, 2 * C)
    row = dft_table(R).transpose(2, 3, 0, 1).reshape(2 * R, 2 * R)
    rest, parts = pfb_window(), []
    for _ in range(3):
        parts.append(rest.astype(ml_dtypes.bfloat16))
        rest = rest - parts[-1].astype(np.float32)
    assert not rest.any()
    parts.append(np.zeros_like(parts[0]))
    return np.concatenate([fine, np.concatenate([column, row], axis=1)] + parts, axis=0)


def kernel(
    volt_hbm, table_hbm, acc,
    volt, window, fine, beam, weighted, send, recv, mid,
    load_sem, table_sem, halo_sem, send_sem, recv_sem,
):
    tm = lax.axis_index("tm")
    me = lax.axis_index("row")
    x, z, core = me // 16, (me // 2) % 8, me % 2
    after, before = (tm + 1) % NTM, (tm + NTM - 1) % NTM

    def partner(e):
        i = e // 4
        dz = 4 + (i + 1) // 2 * (1 - i % 2 * 2)
        dx = 1 - (e // 2) % 2
        dc = 1 - e % 2
        return (((x + dx) % 2) * 8 + (z + dz) % 8) * 2 + (core + dc) % 2

    def load(g):
        return pltpu.make_async_copy(volt_hbm.at[g], volt.at[g + HISTORY], load_sem.at[g])

    def load_half(g, half):
        rows = pl.ds(half * 2 * C, 2 * C)
        return pltpu.make_async_copy(
            volt_hbm.at[g, rows], volt.at[g + HISTORY, rows], load_sem.at[g + FR * half]
        )

    window_copy, fine_copy, beam_copy = [
        pltpu.make_async_copy(table_hbm.at[pl.ds(start, ref.shape[0])], ref, table_sem.at[i])
        for i, (start, ref) in enumerate(
            ((2 * NCH + 2 * C, window), (0, fine), (2 * NCH, beam))
        )
    ]
    window_copy.start()
    for g in range(TAPS):
        load_half(g, 0).start()
    fine_copy.start()

    barrier = pltpu.get_barrier_semaphore()

    def greet(e, carry):
        pl.semaphore_signal(barrier, inc=1, device_id={"row": partner(e)}, device_id_type=MESH_ID)
        return carry

    lax.fori_loop(0, NROW - 1, greet, 0)
    for neighbour in (before, after):
        pl.semaphore_signal(barrier, inc=1, device_id={"tm": neighbour}, device_id_type=MESH_ID)

    for g in range(TAPS):
        load_half(g, 1).start()

    def load_more(g, carry):
        load(g).start()
        return carry

    lax.fori_loop(TAPS, FR, load_more, 0)
    beam_copy.start()

    halo = pltpu.make_async_remote_copy(
        src_ref=volt_hbm.at[pl.ds(FR - HISTORY, HISTORY)],
        dst_ref=volt.at[pl.ds(0, HISTORY)],
        send_sem=halo_sem.at[0],
        recv_sem=halo_sem.at[1],
        device_id={"tm": after},
        device_id_type=MESH_ID,
    )

    def spectrum(g, half):
        parts = window[...].astype(jnp.float32)
        w = parts[:TAPS] + parts[TAPS : 2 * TAPS] + parts[2 * TAPS : 3 * TAPS]

        def chunk(i, carry):
            rows = pl.ds(pl.multiple_of(half * 2 * C + i * 16, 16), 16)
            total = w[0:1] * volt[g, rows, :].astype(jnp.float32)
            for tap in range(1, TAPS):
                total = total + w[tap : tap + 1] * volt[g + tap, rows, :].astype(jnp.float32)
            weighted[rows, :] = total.astype(jnp.bfloat16)
            return carry

        lax.fori_loop(0, 2 * C // 16, chunk, 0, unroll=2)
        out = lax.dot_general(
            fine[...],
            weighted[half * 2 * C : (half + 1) * 2 * C, :],
            (((1,), (1,)), ((), ())),
            preferred_element_type=jnp.float32,
        ).reshape(NROW, 2, KHERE, 2 * C)
        for q in range(2):
            both = jnp.concatenate([out[:, q, :, :C], out[:, q, :, C:]], axis=1)
            send[g, :, half * RK // 2 : (half + 1) * RK // 2, q * C : (q + 1) * C] = (
                both.astype(jnp.bfloat16)
            )

    def dispatch(g, rows):
        def one(e, carry):
            to = partner(e)
            pltpu.make_async_remote_copy(
                src_ref=send.at[g, to, rows],
                dst_ref=recv.at[g, me, rows],
                send_sem=send_sem.at[g],
                recv_sem=recv_sem.at[g],
                device_id={"row": to},
                device_id_type=MESH_ID,
            ).start()
            return carry

        lax.fori_loop(0, NROW - 1, one, 0)
        pltpu.make_async_copy(send.at[g, me, rows], recv.at[g, me, rows], recv_sem.at[g]).start()

    def beams(g):
        pltpu.make_async_copy(send.at[g], recv.at[g], recv_sem.at[g]).wait()
        for part in range(4):
            rows = R * KHERE // 4
            block = recv[g, pl.ds(part * NROW // 4, NROW // 4)].reshape(rows, 2 * C)
            out = jnp.dot(block, beam[:, : 2 * C], preferred_element_type=jnp.float32)
            for q in range(2):
                mid[q, part * rows : (part + 1) * rows, :] = out[:, q * C : (q + 1) * C]
        for pair in range(KHERE // 2):
            sides = []
            for k in (2 * pair, 2 * pair + 1):
                parts = [mid[q, pl.ds(k, R, stride=KHERE), :] for q in range(2)]
                sides.append(jnp.concatenate(parts, axis=0).astype(jnp.bfloat16))
            field = jnp.dot(
                beam[:, 2 * C :], jnp.concatenate(sides, axis=1), preferred_element_type=jnp.float32
            )
            power = (field[:R] * field[:R] + field[R:] * field[R:]) * (1.0 / FR)
            for i in range(2):
                acc[2 * pair + i] += power[:, i * C : (i + 1) * C]

    window_copy.wait()
    for half in range(2):
        for g in range(TAPS):
            load_half(g, half).wait()
        if half == 0:
            fine_copy.wait()
        spectrum(HISTORY, half)
        if half == 0:
            pl.semaphore_wait(barrier, NROW - 1 + 2)
        dispatch(HISTORY, pl.ds(half * RK // 2, RK // 2))
    halo.start()

    def forward(g):
        for half in range(2):
            spectrum(g, half)
        dispatch(g, pl.ds(0, RK))

    def ahead(g, carry):
        load(g).wait()
        forward(g)
        return carry

    lax.fori_loop(TAPS, FR, ahead, 0)
    halo.wait()

    def first(g, carry):
        forward(g)
        return carry

    lax.fori_loop(0, HISTORY, first, 0)

    acc[...] = jnp.zeros_like(acc)
    beam_copy.wait()

    def gather(i, carry):
        beams((i + HISTORY) % FR)
        return carry

    lax.fori_loop(0, FR, gather, 0)

    def sent(g, carry):
        some = pl.ds(0, NROW - 1)
        pltpu.make_async_copy(send.at[g, some], recv.at[g, some], send_sem.at[g]).wait()
        return carry

    lax.fori_loop(0, FR, sent, 0)


def body(voltage):
    frames, rows, columns, width = voltage.shape
    in_hbm = pl.BlockSpec(memory_space=pltpu.HBM)
    power = pl.pallas_call(
        kernel,
        out_shape=jax.ShapeDtypeStruct((KHERE, R, C), jnp.float32),
        in_specs=[in_hbm] * 2,
        out_specs=pl.BlockSpec(memory_space=pltpu.VMEM),
        scratch_shapes=[
            pltpu.VMEM((FR + HISTORY, RHERE * C, 2 * NCH), jnp.bfloat16),
            pltpu.VMEM((4 * TAPS, 2 * NCH), jnp.bfloat16),
            pltpu.VMEM((2 * NCH, 2 * NCH), jnp.bfloat16),
            pltpu.VMEM((2 * C, 4 * C), jnp.bfloat16),
            pltpu.VMEM((RHERE * C, 2 * NCH), jnp.bfloat16),
            pltpu.VMEM((FR, NROW, RK, 2 * C), jnp.bfloat16),
            pltpu.VMEM((FR, NROW, RK, 2 * C), jnp.bfloat16),
            pltpu.VMEM((2, R * KHERE, C), jnp.float32),
            pltpu.SemaphoreType.DMA((FR + HISTORY + 1,)),
            pltpu.SemaphoreType.DMA((3,)),
            pltpu.SemaphoreType.DMA((2,)),
            pltpu.SemaphoreType.DMA((FR,)),
            pltpu.SemaphoreType.DMA((FR,)),
        ],
        compiler_params=pltpu.CompilerParams(
            collective_id=0, has_side_effects=True, vmem_limit_bytes=VMEM_BYTES
        ),
        name="beamformer",
    )(
        voltage.reshape(frames, rows * columns, width),
        jnp.asarray(tables()),
    )
    return power[None]


def solution(mesh):
    return jax.shard_map(
        body,
        mesh=mesh,
        in_specs=(P("tm", "row", None, None),),
        out_specs=P("tm", "row", None, None),
        check_vma=False,
    )
```

```python
import math

import jax
import jax.numpy as jnp
import ml_dtypes
import numpy as np
from jax import lax
from jax.experimental import pallas as pl
from jax.experimental.pallas import tpu as pltpu
from jax.sharding import PartitionSpec as P

TAPS = 4
HISTORY = TAPS - 1
NCH = 256
C = 128
R = 128
FR = 16
NROW = 32
NTM = 8
RHERE = R // NROW
KHERE = NCH // NROW
RK = RHERE * KHERE
VMEM_BYTES = 54656 * 1024
MESH_ID = pl.DeviceIdType.MESH


def pfb_window():
    points = np.arange(TAPS * NCH, dtype=np.float64)
    offset = (points + 0.5) / NCH - TAPS / 2.0
    taper = 0.5 - 0.5 * np.cos(2.0 * math.pi * (points + 0.5) / (TAPS * NCH))
    shaped = (np.sinc(offset) * taper).reshape(TAPS, NCH)
    return np.concatenate([shaped, shaped], axis=1).astype(np.float32)


def dft_table(length):
    indices = np.arange(length)
    angle = (indices[:, None] * indices[None, :] % length) * (2.0 * math.pi / length)
    cosine = np.cos(angle) / math.sqrt(length)
    sine = np.sin(angle) / math.sqrt(length)
    upper = np.stack([cosine, -sine], axis=1)
    bottom = np.stack([sine, cosine], axis=1)
    return np.stack([upper, bottom], axis=0).astype(np.float32).astype(ml_dtypes.bfloat16)


def tables():
    fine = dft_table(NCH).reshape(2 * NCH, 2, NROW, KHERE).transpose(2, 1, 3, 0)
    fine = fine.reshape(2 * NCH, 2 * NCH)
    column = dft_table(C).reshape(2 * C, 2 * C)
    row = dft_table(R).transpose(2, 3, 0, 1).reshape(2 * R, 2 * R)
    rest, parts = pfb_window(), []
    for _ in range(3):
        parts.append(rest.astype(ml_dtypes.bfloat16))
        rest = rest - parts[-1].astype(np.float32)
    assert not rest.any()
    parts.append(np.zeros_like(parts[0]))
    return np.concatenate([fine, np.concatenate([column, row], axis=1)] + parts, axis=0)


def kernel(
    volt_hbm, table_hbm, acc,
    volt, window, fine, beam, weighted, send, recv, mid,
    load_sem, table_sem, halo_sem, send_sem, recv_sem, go_sem,
):
    tm = lax.axis_index("tm")
    me = lax.axis_index("row")
    x, z, core = me // 16, (me // 2) % 8, me % 2
    after, before = (tm + 1) % NTM, (tm + NTM - 1) % NTM

    def partner(e):
        i = e // 4
        dz = 4 + (i + 1) // 2 * (1 - i % 2 * 2)
        dx = 1 - (e // 2) % 2
        dc = 1 - e % 2
        return (((x + dx) % 2) * 8 + (z + dz) % 8) * 2 + (core + dc) % 2

    def load(g):
        return pltpu.make_async_copy(volt_hbm.at[g], volt.at[g + HISTORY], load_sem.at[g])

    def load_half(g, half):
        rows = pl.ds(half * 2 * C, 2 * C)
        return pltpu.make_async_copy(
            volt_hbm.at[g, rows], volt.at[g + HISTORY, rows], load_sem.at[g + FR * half]
        )

    window_copy, fine_copy, beam_copy = [
        pltpu.make_async_copy(table_hbm.at[pl.ds(start, ref.shape[0])], ref, table_sem.at[i])
        for i, (start, ref) in enumerate(
            ((2 * NCH + 2 * C, window), (0, fine), (2 * NCH, beam))
        )
    ]
    window_copy.start()
    for g in range(TAPS):
        load_half(g, 0).start()
    fine_copy.start()

    barrier = pltpu.get_barrier_semaphore()

    def signal(sem, **device_id):
        pl.semaphore_signal(sem, inc=1, device_id=device_id, device_id_type=MESH_ID)

    def greet(e, carry):
        signal(barrier, row=partner(2 * e + 1) // 2 * 2)
        return carry

    lax.fori_loop(0, NROW // 2 - 1, greet, 0)

    @pl.when(core == 1)
    def _():
        signal(barrier, row=me - 1)

    for g in range(TAPS):
        load_half(g, 1).start()

    def load_more(g, carry):
        load(g).start()
        return carry

    lax.fori_loop(TAPS, FR, load_more, 0)
    beam_copy.start()

    halo = pltpu.make_async_remote_copy(
        src_ref=volt_hbm.at[pl.ds(FR - HISTORY, HISTORY)],
        dst_ref=volt.at[pl.ds(0, HISTORY)],
        send_sem=halo_sem.at[0],
        recv_sem=halo_sem.at[1],
        device_id={"tm": after},
        device_id_type=MESH_ID,
    )

    def spectrum(g, half):
        parts = window[...].astype(jnp.float32)
        w = parts[:TAPS] + parts[TAPS : 2 * TAPS] + parts[2 * TAPS : 3 * TAPS]

        def chunk(i, carry):
            rows = pl.ds(pl.multiple_of(half * 2 * C + i * 16, 16), 16)
            total = w[0:1] * volt[g, rows, :].astype(jnp.float32)
            for tap in range(1, TAPS):
                total = total + w[tap : tap + 1] * volt[g + tap, rows, :].astype(jnp.float32)
            weighted[rows, :] = total.astype(jnp.bfloat16)
            return carry

        lax.fori_loop(0, 2 * C // 16, chunk, 0, unroll=2)
        out = lax.dot_general(
            fine[...],
            weighted[half * 2 * C : (half + 1) * 2 * C, :],
            (((1,), (1,)), ((), ())),
            preferred_element_type=jnp.float32,
        ).reshape(NROW, 2, KHERE, 2 * C)
        for q in range(2):
            both = jnp.concatenate([out[:, q, :, :C], out[:, q, :, C:]], axis=1)
            send[g, :, half * RK // 2 : (half + 1) * RK // 2, q * C : (q + 1) * C] = (
                both.astype(jnp.bfloat16)
            )

    def dispatch(g, rows):
        def one(e, carry):
            to = partner(e)
            pltpu.make_async_remote_copy(
                src_ref=send.at[g, to, rows],
                dst_ref=recv.at[g, me, rows],
                send_sem=send_sem.at[g],
                recv_sem=recv_sem.at[g],
                device_id={"row": to},
                device_id_type=MESH_ID,
            ).start()
            return carry

        lax.fori_loop(0, NROW - 1, one, 0)
        pltpu.make_async_copy(send.at[g, me, rows], recv.at[g, me, rows], recv_sem.at[g]).start()

    def beams(g):
        pltpu.make_async_copy(send.at[g], recv.at[g], recv_sem.at[g]).wait()
        for part in range(4):
            rows = R * KHERE // 4
            block = recv[g, pl.ds(part * NROW // 4, NROW // 4)].reshape(rows, 2 * C)
            out = jnp.dot(block, beam[:, : 2 * C], preferred_element_type=jnp.float32)
            for q in range(2):
                mid[q, part * rows : (part + 1) * rows, :] = out[:, q * C : (q + 1) * C]
        for pair in range(KHERE // 2):
            sides = []
            for k in (2 * pair, 2 * pair + 1):
                parts = [mid[q, pl.ds(k, R, stride=KHERE), :] for q in range(2)]
                sides.append(jnp.concatenate(parts, axis=0).astype(jnp.bfloat16))
            field = jnp.dot(
                beam[:, 2 * C :], jnp.concatenate(sides, axis=1), preferred_element_type=jnp.float32
            )
            power = (field[:R] * field[:R] + field[R:] * field[R:]) * (1.0 / FR)
            for i in range(2):
                acc[2 * pair + i] += power[:, i * C : (i + 1) * C]

    def enter():
        @pl.when(core == 0)
        def _():
            pl.semaphore_wait(barrier, NROW - 1)
            signal(go_sem.at[0], row=me + 1)

        @pl.when(core == 1)
        def _():
            pl.semaphore_wait(go_sem.at[0], 1)
            signal(barrier, tm=before)

    def meet_next_slab():
        @pl.when(core == 1)
        def _():
            pl.semaphore_wait(barrier, 1)
            signal(go_sem.at[1], row=me - 1)

        @pl.when(core == 0)
        def _():
            pl.semaphore_wait(go_sem.at[1], 1)

    window_copy.wait()
    for half in range(2):
        for g in range(TAPS):
            load_half(g, half).wait()
        if half == 0:
            fine_copy.wait()
        spectrum(HISTORY, half)
        if half == 0:
            enter()
        dispatch(HISTORY, pl.ds(half * RK // 2, RK // 2))

    def forward(g):
        for half in range(2):
            spectrum(g, half)
        dispatch(g, pl.ds(0, RK))

    def ahead(g, carry):
        load(g).wait()
        forward(g)
        return carry

    lax.fori_loop(TAPS, TAPS + 2, ahead, 0)
    meet_next_slab()
    halo.start()
    lax.fori_loop(TAPS + 2, FR, ahead, 0)
    halo.wait()

    def first(g, carry):
        forward(g)
        return carry

    lax.fori_loop(0, HISTORY, first, 0)

    acc[...] = jnp.zeros_like(acc)
    beam_copy.wait()

    def gather(i, carry):
        beams((i + HISTORY) % FR)
        return carry

    lax.fori_loop(0, FR, gather, 0)

    def sent(g, carry):
        some = pl.ds(0, NROW - 1)
        pltpu.make_async_copy(send.at[g, some], recv.at[g, some], send_sem.at[g]).wait()
        return carry

    lax.fori_loop(0, FR, sent, 0)


def body(voltage):
    frames, rows, columns, width = voltage.shape
    in_hbm = pl.BlockSpec(memory_space=pltpu.HBM)
    power = pl.pallas_call(
        kernel,
        out_shape=jax.ShapeDtypeStruct((KHERE, R, C), jnp.float32),
        in_specs=[in_hbm] * 2,
        out_specs=pl.BlockSpec(memory_space=pltpu.VMEM),
        scratch_shapes=[
            pltpu.VMEM((FR + HISTORY, RHERE * C, 2 * NCH), jnp.bfloat16),
            pltpu.VMEM((4 * TAPS, 2 * NCH), jnp.bfloat16),
            pltpu.VMEM((2 * NCH, 2 * NCH), jnp.bfloat16),
            pltpu.VMEM((2 * C, 4 * C), jnp.bfloat16),
            pltpu.VMEM((RHERE * C, 2 * NCH), jnp.bfloat16),
            pltpu.VMEM((FR, NROW, RK, 2 * C), jnp.bfloat16),
            pltpu.VMEM((FR, NROW, RK, 2 * C), jnp.bfloat16),
            pltpu.VMEM((2, R * KHERE, C), jnp.float32),
            pltpu.SemaphoreType.DMA((FR + HISTORY + 1,)),
            pltpu.SemaphoreType.DMA((3,)),
            pltpu.SemaphoreType.DMA((2,)),
            pltpu.SemaphoreType.DMA((FR,)),
            pltpu.SemaphoreType.DMA((FR,)),
            pltpu.SemaphoreType.REGULAR((2,)),
        ],
        compiler_params=pltpu.CompilerParams(
            collective_id=0, has_side_effects=True, vmem_limit_bytes=VMEM_BYTES
        ),
        name="beamformer",
    )(
        voltage.reshape(frames, rows * columns, width),
        jnp.asarray(tables()),
    )
    return power[None]


def solution(mesh):
    return jax.shard_map(
        body,
        mesh=mesh,
        in_specs=(P("tm", "row", None, None),),
        out_specs=P("tm", "row", None, None),
        check_vma=False,
    )
```

```python
import math

import jax
import jax.numpy as jnp
import ml_dtypes
import numpy as np
from jax import lax
from jax.experimental import pallas as pl
from jax.experimental.pallas import tpu as pltpu
from jax.sharding import PartitionSpec as P

TAPS = 4
HISTORY = TAPS - 1
NCH = 256
C = 128
R = 128
FR = 16
NROW = 32
NTM = 8
RHERE = R // NROW
KHERE = NCH // NROW
RK = RHERE * KHERE
PARTS = 4
PART = NROW // PARTS
FAR = 5
VMEM_BYTES = 54656 * 1024
MESH_ID = pl.DeviceIdType.MESH


def pfb_window():
    points = np.arange(TAPS * NCH, dtype=np.float64)
    offset = (points + 0.5) / NCH - TAPS / 2.0
    taper = 0.5 - 0.5 * np.cos(2.0 * math.pi * (points + 0.5) / (TAPS * NCH))
    shaped = (np.sinc(offset) * taper).reshape(TAPS, NCH)
    return np.concatenate([shaped, shaped], axis=1).astype(np.float32)


def dft_table(length):
    indices = np.arange(length)
    angle = (indices[:, None] * indices[None, :] % length) * (2.0 * math.pi / length)
    cosine = np.cos(angle) / math.sqrt(length)
    sine = np.sin(angle) / math.sqrt(length)
    upper = np.stack([cosine, -sine], axis=1)
    bottom = np.stack([sine, cosine], axis=1)
    return np.stack([upper, bottom], axis=0).astype(np.float32).astype(ml_dtypes.bfloat16)


def tables():
    fine = dft_table(NCH).reshape(2 * NCH, 2, NROW, KHERE).transpose(2, 1, 3, 0)
    fine = fine.reshape(2 * NCH, 2 * NCH)
    column = dft_table(C).reshape(2 * C, 2 * C)
    row = dft_table(R).transpose(2, 3, 0, 1).reshape(2 * R, 2 * R)
    rest, parts = pfb_window(), []
    for _ in range(3):
        parts.append(rest.astype(ml_dtypes.bfloat16))
        rest = rest - parts[-1].astype(np.float32)
    assert not rest.any()
    parts.append(np.zeros_like(parts[0]))
    return np.concatenate([fine, np.concatenate([column, row], axis=1)] + parts, axis=0)


def kernel(
    volt_hbm, table_hbm, acc,
    volt, window, fine, beam, weighted, send, recv, mid,
    load_sem, table_sem, halo_sem, send_sem, recv_sem, go_sem,
):
    tm = lax.axis_index("tm")
    me = lax.axis_index("row")
    x, z, core = me // 16, (me // 2) % 8, me % 2
    after, before = (tm + 1) % NTM, (tm + NTM - 1) % NTM

    def plane(i):
        return (z + 4 + (i + 1) // 2 * (1 - i % 2 * 2)) % 8

    half_ring = NROW // 2

    def device(there, dx, dc):
        return (x if dx == 0 else 1 - x) * half_ring + 2 * there + (core if dc == 0 else 1 - core)

    SPOTS = ((1, 1), (1, 0), (0, 1), (0, 0))

    def load(g):
        return pltpu.make_async_copy(volt_hbm.at[g], volt.at[g + HISTORY], load_sem.at[g])

    def load_half(g, half):
        rows = pl.ds(half * 2 * C, 2 * C)
        return pltpu.make_async_copy(
            volt_hbm.at[g, rows], volt.at[g + HISTORY, rows], load_sem.at[g + FR * half]
        )

    window_copy, *fine_copies, beam_copy = [
        pltpu.make_async_copy(table_hbm.at[pl.ds(start, ref.shape[0])], ref, table_sem.at[i])
        for i, (start, ref) in enumerate(
            (
                (2 * NCH + 2 * C, window),
                (0, fine.at[pl.ds(0, NCH)]),
                (NCH, fine.at[pl.ds(NCH, NCH)]),
                (2 * NCH, beam),
            )
        )
    ]
    window_copy.start()
    for g in range(TAPS):
        load_half(g, 0).start()
    for copy in fine_copies:
        copy.start()

    barrier = pltpu.get_barrier_semaphore()
    near_ear, slab_ear = 2 * z + 1, NROW // 2 + 2 * z + 1
    is_near_ear, is_slab_ear = me == near_ear, me == slab_ear

    def signal(sem, **device_id):
        pl.semaphore_signal(sem, inc=1, device_id=device_id, device_id_type=MESH_ID)

    def tell_plane(sem, ear):
        chip = ear - 1
        signal(sem, row=chip)
        signal(sem, row=(chip + NROW // 2) % NROW)
        signal(sem, row=(ear + NROW // 2) % NROW)

    def greet(i, carry):
        there = plane(i)
        for side in range(2):
            signal(barrier, row=side * half_ring + 2 * there)
        return carry

    for dz in (1, 7):
        signal(barrier, row=2 * ((z + dz) % 8) + 1)

    @pl.when(jnp.logical_not(is_near_ear))
    def _():
        signal(barrier, row=near_ear)

    @pl.when(core == 1)
    def _():
        signal(barrier, row=me - 1)

    signal(barrier, row=(1 - x) * half_ring + 2 * z)
    lax.fori_loop(0, 7, greet, 0)

    for g in range(TAPS):
        load_half(g, 1).start()

    def load_more(g, carry):
        load(g).start()
        return carry

    lax.fori_loop(TAPS, FR, load_more, 0)
    beam_copy.start()

    halo = pltpu.make_async_remote_copy(
        src_ref=volt_hbm.at[pl.ds(FR - HISTORY, HISTORY)],
        dst_ref=volt.at[pl.ds(0, HISTORY)],
        send_sem=halo_sem.at[0],
        recv_sem=halo_sem.at[1],
        device_id={"tm": after},
        device_id_type=MESH_ID,
    )

    everything = pl.ds(0, RK)

    def half_of_block(half):
        return pl.ds(pl.multiple_of(half * (RK // 2), RK // 2), RK // 2)

    def spectrum(g, half):
        parts = window[...].astype(jnp.float32)
        w = parts[:TAPS] + parts[TAPS : 2 * TAPS] + parts[2 * TAPS : 3 * TAPS]

        def chunk(i, carry):
            rows = pl.ds(pl.multiple_of(half * 2 * C + i * 16, 16), 16)
            total = w[0:1] * volt[g, rows, :].astype(jnp.float32)
            for tap in range(1, TAPS):
                total = total + w[tap : tap + 1] * volt[g + tap, rows, :].astype(jnp.float32)
            weighted[pl.ds(pl.multiple_of(i * 16, 16), 16), :] = total.astype(jnp.bfloat16)
            return carry

        lax.fori_loop(0, 2 * C // 16, chunk, 0, unroll=2)
        out = lax.dot_general(
            fine[...],
            weighted[...],
            (((1,), (1,)), ((), ())),
            preferred_element_type=jnp.float32,
        ).reshape(NROW, 2, KHERE, 2 * C)
        for q in range(2):
            both = jnp.concatenate([out[:, q, :, :C], out[:, q, :, C:]], axis=1)
            send[g, :, half_of_block(half), q * C : (q + 1) * C] = both.astype(jnp.bfloat16)

    def dispatch(g, rows, start, end):
        def post(to):
            pltpu.make_async_remote_copy(
                src_ref=send.at[g, to, rows],
                dst_ref=recv.at[g, me, rows],
                send_sem=send_sem.at[g],
                recv_sem=recv_sem.at[g],
                device_id={"row": to},
                device_id_type=MESH_ID,
            ).start()

        def one(i, carry):
            there = plane(i)
            for dx, dc in SPOTS:
                post(device(there, dx, dc))
            return carry

        lax.fori_loop(start, min(end, 7), one, 0)
        if end == 8:
            for dx, dc in SPOTS[:3]:
                post(device(z, dx, dc))

    def keep(g):
        pltpu.make_async_copy(
            send.at[g, me], recv.at[g, me], recv_sem.at[g]
        ).start()

    def beams(g):
        pltpu.make_async_copy(send.at[g], recv.at[g], recv_sem.at[g]).wait()
        for part in range(PARTS):
            rows = R * KHERE // PARTS
            sources = pl.ds(part * PART, PART)
            block = recv[g, sources].reshape(rows, 2 * C)
            out = jnp.dot(block, beam[:, : 2 * C], preferred_element_type=jnp.float32)
            for q in range(2):
                mid[q, part * rows : (part + 1) * rows, :] = out[:, q * C : (q + 1) * C]
        for pair in range(KHERE // 2):
            sides = []
            for k in (2 * pair, 2 * pair + 1):
                parts = [mid[q, pl.ds(k, R, stride=KHERE), :] for q in range(2)]
                sides.append(jnp.concatenate(parts, axis=0).astype(jnp.bfloat16))
            field = jnp.dot(
                beam[:, 2 * C :], jnp.concatenate(sides, axis=1), preferred_element_type=jnp.float32
            )
            power = (field[:R] * field[:R] + field[R:] * field[R:]) * (1.0 / FR)
            for i in range(2):
                acc[2 * pair + i] += power[:, i * C : (i + 1) * C]

    def enter_near():
        @pl.when(is_near_ear)
        def _():
            pl.semaphore_wait(barrier, 3 + 2 * 4)
            tell_plane(go_sem.at[0], near_ear)

        @pl.when(jnp.logical_not(is_near_ear))
        def _():
            pl.semaphore_wait(go_sem.at[0], 1)

    def enter():
        @pl.when(core == 0)
        def _():
            pl.semaphore_wait(barrier, NROW - 1)
            signal(go_sem.at[1], row=me + 1)

        @pl.when(core == 1)
        def _():
            pl.semaphore_wait(go_sem.at[1], 1)

        @pl.when(is_slab_ear)
        def _():
            signal(barrier, tm=before)

    def meet_next_slab():
        @pl.when(is_slab_ear)
        def _():
            pl.semaphore_wait(barrier, 1)
            tell_plane(go_sem.at[2], slab_ear)

        @pl.when(jnp.logical_not(is_slab_ear))
        def _():
            pl.semaphore_wait(go_sem.at[2], 1)

    acc[...] = jnp.zeros_like(acc)

    def produce(n, carry):
        g, half = (n // 2 + HISTORY) % FR, n % 2

        @pl.when(n == 0)
        def _():
            window_copy.wait()
            for i in range(TAPS):
                load_half(i, 0).wait()
            for copy in fine_copies:
                copy.wait()

        @pl.when(n == 1)
        def _():
            for i in range(TAPS):
                load_half(i, 1).wait()

        @pl.when((n > 1) & (half == 0) & (g >= TAPS))
        def _():
            load(g).wait()

        @pl.when(n == 2 * (FR - HISTORY))
        def _():
            halo.wait()

        spectrum(g, half)

        @pl.when(n == 0)
        def _():
            enter_near()

        @pl.when(n < 4)
        def _():
            dispatch(g, half_of_block(half), FAR, 8)

        @pl.when(n == 3)
        def _():
            enter()

            def rest(f, carry):
                dispatch(f, everything, 0, FAR)
                keep(f)
                return carry

            lax.fori_loop(HISTORY, HISTORY + 2, rest, 0)

        @pl.when((n > 3) & (half == 1))
        def _():
            dispatch(g, everything, 0, 8)
            keep(g)

        @pl.when(n == 7)
        def _():
            meet_next_slab()
            halo.start()

        return carry

    lax.fori_loop(0, 2 * FR, produce, 0)
    beam_copy.wait()

    def sent(g):
        some = pl.ds(0, NROW - 1)
        pltpu.make_async_copy(send.at[g, some], recv.at[g, some], send_sem.at[g]).wait()

    def gather(i, carry):
        beams((i + HISTORY) % FR)

        @pl.when(i < FR - 1)
        def _():
            sent((i + HISTORY) % FR)

        return carry

    lax.fori_loop(0, FR, gather, 0)
    sent(HISTORY - 1)


def body(voltage):
    frames, rows, columns, width = voltage.shape
    in_hbm = pl.BlockSpec(memory_space=pltpu.HBM)
    power = pl.pallas_call(
        kernel,
        out_shape=jax.ShapeDtypeStruct((KHERE, R, C), jnp.float32),
        in_specs=[in_hbm] * 2,
        out_specs=pl.BlockSpec(memory_space=pltpu.VMEM),
        scratch_shapes=[
            pltpu.VMEM((FR + HISTORY, RHERE * C, 2 * NCH), jnp.bfloat16),
            pltpu.VMEM((4 * TAPS, 2 * NCH), jnp.bfloat16),
            pltpu.VMEM((2 * NCH, 2 * NCH), jnp.bfloat16),
            pltpu.VMEM((2 * C, 4 * C), jnp.bfloat16),
            pltpu.VMEM((RHERE * C // 2, 2 * NCH), jnp.bfloat16),
            pltpu.VMEM((FR, NROW, RK, 2 * C), jnp.bfloat16),
            pltpu.VMEM((FR, NROW, RK, 2 * C), jnp.bfloat16),
            pltpu.VMEM((2, R * KHERE, C), jnp.float32),
            pltpu.SemaphoreType.DMA((FR + HISTORY + 1,)),
            pltpu.SemaphoreType.DMA((4,)),
            pltpu.SemaphoreType.DMA((2,)),
            pltpu.SemaphoreType.DMA((FR,)),
            pltpu.SemaphoreType.DMA((FR,)),
            pltpu.SemaphoreType.REGULAR((3,)),
        ],
        compiler_params=pltpu.CompilerParams(
            collective_id=0, has_side_effects=True, vmem_limit_bytes=VMEM_BYTES
        ),
        name="beamformer",
    )(
        voltage.reshape(frames, rows * columns, width),
        jnp.asarray(tables()),
    )
    return power[None]


def solution(mesh):
    return jax.shard_map(
        body,
        mesh=mesh,
        in_specs=(P("tm", "row", None, None),),
        out_specs=P("tm", "row", None, None),
        check_vma=False,
    )
```

```python
import math

import jax
import jax.numpy as jnp
import ml_dtypes
import numpy as np
from jax import lax
from jax.experimental import pallas as pl
from jax.experimental.pallas import tpu as pltpu
from jax.sharding import PartitionSpec as P

TAPS = 4
HISTORY = TAPS - 1
NCH = 256
C = 128
R = 128
FR = 16
NROW = 32
NTM = 8
RHERE = R // NROW
KHERE = NCH // NROW
RK = RHERE * KHERE
PARTS = 4
PART = NROW // PARTS
FAR = 5
VMEM_BYTES = 54656 * 1024
MESH_ID = pl.DeviceIdType.MESH


def pfb_window():
    points = np.arange(TAPS * NCH, dtype=np.float64)
    offset = (points + 0.5) / NCH - TAPS / 2.0
    taper = 0.5 - 0.5 * np.cos(2.0 * math.pi * (points + 0.5) / (TAPS * NCH))
    shaped = (np.sinc(offset) * taper).reshape(TAPS, NCH)
    return np.concatenate([shaped, shaped], axis=1).astype(np.float32)


def dft_table(length):
    indices = np.arange(length)
    angle = (indices[:, None] * indices[None, :] % length) * (2.0 * math.pi / length)
    cosine = np.cos(angle) / math.sqrt(length)
    sine = np.sin(angle) / math.sqrt(length)
    upper = np.stack([cosine, -sine], axis=1)
    bottom = np.stack([sine, cosine], axis=1)
    return np.stack([upper, bottom], axis=0).astype(np.float32).astype(ml_dtypes.bfloat16)


def tables():
    fine = dft_table(NCH).reshape(2 * NCH, 2, NROW, KHERE).transpose(2, 1, 3, 0)
    fine = fine.reshape(2 * NCH, 2 * NCH)
    column = dft_table(C).reshape(2 * C, 2 * C)
    row = dft_table(R).transpose(2, 3, 0, 1).reshape(2 * R, 2 * R)
    rest, parts = pfb_window(), []
    for _ in range(3):
        parts.append(rest.astype(ml_dtypes.bfloat16))
        rest = rest - parts[-1].astype(np.float32)
    assert not rest.any()
    parts.append(np.zeros_like(parts[0]))
    return np.concatenate([fine, np.concatenate([column, row], axis=1)] + parts, axis=0)


def kernel(
    volt_hbm, table_hbm, acc,
    volt, window, fine, beam, weighted, send, recv, mid,
    load_sem, table_sem, halo_sem, send_sem, recv_sem, go_sem,
):
    tm = lax.axis_index("tm")
    me = lax.axis_index("row")
    x, z, core = me // 16, (me // 2) % 8, me % 2
    after, before = (tm + 1) % NTM, (tm + NTM - 1) % NTM

    def plane(i):
        return (z + 4 + (i + 1) // 2 * (1 - i % 2 * 2)) % 8

    half_ring = NROW // 2

    def device(there, dx, dc):
        return (x if dx == 0 else 1 - x) * half_ring + 2 * there + (core if dc == 0 else 1 - core)

    SPOTS = ((1, 1), (1, 0), (0, 1), (0, 0))

    def load(g):
        return pltpu.make_async_copy(volt_hbm.at[g], volt.at[g + HISTORY], load_sem.at[g])

    def load_half(g, half):
        rows = pl.ds(half * 2 * C, 2 * C)
        return pltpu.make_async_copy(
            volt_hbm.at[g, rows], volt.at[g + HISTORY, rows], load_sem.at[g + FR * half]
        )

    window_copy, *fine_copies, beam_copy = [
        pltpu.make_async_copy(table_hbm.at[pl.ds(start, ref.shape[0])], ref, table_sem.at[i])
        for i, (start, ref) in enumerate(
            (
                (2 * NCH + 2 * C, window),
                (0, fine.at[pl.ds(0, NCH)]),
                (NCH, fine.at[pl.ds(NCH, NCH)]),
                (2 * NCH, beam),
            )
        )
    ]
    window_copy.start()
    for g in range(TAPS):
        load_half(g, 0).start()
    for copy in fine_copies:
        copy.start()

    barrier = pltpu.get_barrier_semaphore()
    near_ear, slab_ear = 2 * z + 1, NROW // 2 + 2 * z + 1
    is_near_ear, is_slab_ear = me == near_ear, me == slab_ear

    def signal(sem, **device_id):
        pl.semaphore_signal(sem, inc=1, device_id=device_id, device_id_type=MESH_ID)

    def tell_plane(sem, ear):
        chip = ear - 1
        signal(sem, row=chip)
        signal(sem, row=(chip + NROW // 2) % NROW)
        signal(sem, row=(ear + NROW // 2) % NROW)

    def greet(i, carry):
        there = plane(i)
        for side in range(2):
            signal(barrier, row=side * half_ring + 2 * there)
        return carry

    for dz in (1, 7):
        signal(barrier, row=2 * ((z + dz) % 8) + 1)

    @pl.when(jnp.logical_not(is_near_ear))
    def _():
        signal(barrier, row=near_ear)

    @pl.when(core == 1)
    def _():
        signal(barrier, row=me - 1)

    signal(barrier, row=(1 - x) * half_ring + 2 * z)
    lax.fori_loop(0, 7, greet, 0)

    for g in range(TAPS):
        load_half(g, 1).start()

    def load_more(g, carry):
        load(g).start()
        return carry

    lax.fori_loop(TAPS, FR, load_more, 0)
    beam_copy.start()

    halo = pltpu.make_async_remote_copy(
        src_ref=volt_hbm.at[pl.ds(FR - HISTORY, HISTORY)],
        dst_ref=volt.at[pl.ds(0, HISTORY)],
        send_sem=halo_sem.at[0],
        recv_sem=halo_sem.at[1],
        device_id={"tm": after},
        device_id_type=MESH_ID,
    )

    everything = pl.ds(0, RK)

    def half_of_block(half):
        return pl.ds(pl.multiple_of(half * (RK // 2), RK // 2), RK // 2)

    def spectrum(g, half, before_transform):
        parts = window[...].astype(jnp.float32)
        w = parts[:TAPS] + parts[TAPS : 2 * TAPS] + parts[2 * TAPS : 3 * TAPS]

        def chunk(i, carry):
            rows = pl.ds(pl.multiple_of(half * 2 * C + i * 16, 16), 16)
            total = w[0:1] * volt[g, rows, :].astype(jnp.float32)
            for tap in range(1, TAPS):
                total = total + w[tap : tap + 1] * volt[g + tap, rows, :].astype(jnp.float32)
            weighted[pl.ds(pl.multiple_of(i * 16, 16), 16), :] = total.astype(jnp.bfloat16)
            return carry

        lax.fori_loop(0, 2 * C // 16, chunk, 0, unroll=2)
        before_transform()
        out = lax.dot_general(
            fine[...],
            weighted[...],
            (((1,), (1,)), ((), ())),
            preferred_element_type=jnp.float32,
        ).reshape(NROW, 2, KHERE, 2 * C)
        for q in range(2):
            both = jnp.concatenate([out[:, q, :, :C], out[:, q, :, C:]], axis=1)
            send[g, :, half_of_block(half), q * C : (q + 1) * C] = both.astype(jnp.bfloat16)

    def dispatch(g, rows, start, end):
        def post(to):
            pltpu.make_async_remote_copy(
                src_ref=send.at[g, to, rows],
                dst_ref=recv.at[g, me, rows],
                send_sem=send_sem.at[g],
                recv_sem=recv_sem.at[g],
                device_id={"row": to},
                device_id_type=MESH_ID,
            ).start()

        def one(i, carry):
            there = plane(i)
            for dx, dc in SPOTS:
                post(device(there, dx, dc))
            return carry

        lax.fori_loop(start, min(end, 7), one, 0)
        if end == 8:
            for dx, dc in SPOTS[:3]:
                post(device(z, dx, dc))

    def keep(g):
        pltpu.make_async_copy(
            send.at[g, me], recv.at[g, me], recv_sem.at[g]
        ).start()

    def beams(g):
        pltpu.make_async_copy(send.at[g], recv.at[g], recv_sem.at[g]).wait()
        for part in range(PARTS):
            rows = R * KHERE // PARTS
            sources = pl.ds(part * PART, PART)
            block = recv[g, sources].reshape(rows, 2 * C)
            out = jnp.dot(block, beam[:, : 2 * C], preferred_element_type=jnp.float32)
            for q in range(2):
                mid[q, part * rows : (part + 1) * rows, :] = out[:, q * C : (q + 1) * C]
        for pair in range(KHERE // 2):
            sides = []
            for k in (2 * pair, 2 * pair + 1):
                parts = [mid[q, pl.ds(k, R, stride=KHERE), :] for q in range(2)]
                sides.append(jnp.concatenate(parts, axis=0).astype(jnp.bfloat16))
            field = jnp.dot(
                beam[:, 2 * C :], jnp.concatenate(sides, axis=1), preferred_element_type=jnp.float32
            )
            power = (field[:R] * field[:R] + field[R:] * field[R:]) * (1.0 / FR)
            for i in range(2):
                acc[2 * pair + i] += power[:, i * C : (i + 1) * C]

    def relay_near():
        @pl.when(is_near_ear)
        def _():
            pl.semaphore_wait(barrier, 3 + 2 * 4)
            tell_plane(go_sem.at[0], near_ear)

    def enter_near():
        @pl.when(jnp.logical_not(is_near_ear))
        def _():
            pl.semaphore_wait(go_sem.at[0], 1)

    def enter():
        @pl.when(core == 0)
        def _():
            pl.semaphore_wait(barrier, NROW - 1)
            signal(go_sem.at[1], row=me + 1)

        @pl.when(core == 1)
        def _():
            pl.semaphore_wait(go_sem.at[1], 1)

        @pl.when(is_slab_ear)
        def _():
            signal(barrier, tm=before)

    def meet_next_slab():
        @pl.when(is_slab_ear)
        def _():
            pl.semaphore_wait(barrier, 1)
            tell_plane(go_sem.at[2], slab_ear)

        @pl.when(jnp.logical_not(is_slab_ear))
        def _():
            pl.semaphore_wait(go_sem.at[2], 1)

    acc[...] = jnp.zeros_like(acc)

    def produce(n, carry):
        g, half = (n // 2 + HISTORY) % FR, n % 2

        @pl.when(n == 0)
        def _():
            window_copy.wait()
            for i in range(TAPS):
                load_half(i, 0).wait()
            relay_near()

        @pl.when(n == 1)
        def _():
            for i in range(TAPS):
                load_half(i, 1).wait()

        @pl.when((n > 1) & (half == 0) & (g >= TAPS))
        def _():
            load(g).wait()

        @pl.when(n == 2 * (FR - HISTORY))
        def _():
            halo.wait()

        def fine_ready():
            @pl.when(n == 0)
            def _():
                for copy in fine_copies:
                    copy.wait()

        spectrum(g, half, fine_ready)

        @pl.when(n == 0)
        def _():
            enter_near()

        @pl.when(n < 4)
        def _():
            dispatch(g, half_of_block(half), FAR, 8)

        @pl.when(n == 3)
        def _():
            enter()

            def rest(f, carry):
                dispatch(f, everything, 0, FAR)
                keep(f)
                return carry

            lax.fori_loop(HISTORY, HISTORY + 2, rest, 0)

        @pl.when((n > 3) & (half == 1))
        def _():
            dispatch(g, everything, 0, 8)
            keep(g)

        @pl.when(n == 7)
        def _():
            meet_next_slab()
            halo.start()

        return carry

    lax.fori_loop(0, 2 * FR, produce, 0)
    beam_copy.wait()

    def sent(g):
        some = pl.ds(0, NROW - 1)
        pltpu.make_async_copy(send.at[g, some], recv.at[g, some], send_sem.at[g]).wait()

    def gather(i, carry):
        beams((i + HISTORY) % FR)

        @pl.when(i < FR - 1)
        def _():
            sent((i + HISTORY) % FR)

        return carry

    lax.fori_loop(0, FR, gather, 0)
    sent(HISTORY - 1)


def body(voltage):
    frames, rows, columns, width = voltage.shape
    in_hbm = pl.BlockSpec(memory_space=pltpu.HBM)
    power = pl.pallas_call(
        kernel,
        out_shape=jax.ShapeDtypeStruct((KHERE, R, C), jnp.float32),
        in_specs=[in_hbm] * 2,
        out_specs=pl.BlockSpec(memory_space=pltpu.VMEM),
        scratch_shapes=[
            pltpu.VMEM((FR + HISTORY, RHERE * C, 2 * NCH), jnp.bfloat16),
            pltpu.VMEM((4 * TAPS, 2 * NCH), jnp.bfloat16),
            pltpu.VMEM((2 * NCH, 2 * NCH), jnp.bfloat16),
            pltpu.VMEM((2 * C, 4 * C), jnp.bfloat16),
            pltpu.VMEM((RHERE * C // 2, 2 * NCH), jnp.bfloat16),
            pltpu.VMEM((FR, NROW, RK, 2 * C), jnp.bfloat16),
            pltpu.VMEM((FR, NROW, RK, 2 * C), jnp.bfloat16),
            pltpu.VMEM((2, R * KHERE, C), jnp.float32),
            pltpu.SemaphoreType.DMA((FR + HISTORY + 1,)),
            pltpu.SemaphoreType.DMA((4,)),
            pltpu.SemaphoreType.DMA((2,)),
            pltpu.SemaphoreType.DMA((FR,)),
            pltpu.SemaphoreType.DMA((FR,)),
            pltpu.SemaphoreType.REGULAR((3,)),
        ],
        compiler_params=pltpu.CompilerParams(
            collective_id=0, has_side_effects=True, vmem_limit_bytes=VMEM_BYTES
        ),
        name="beamformer",
    )(
        voltage.reshape(frames, rows * columns, width),
        jnp.asarray(tables()),
    )
    return power[None]


def solution(mesh):
    return jax.shard_map(
        body,
        mesh=mesh,
        in_specs=(P("tm", "row", None, None),),
        out_specs=P("tm", "row", None, None),
        check_vma=False,
    )
```

```python
import math

import jax
import jax.numpy as jnp
import ml_dtypes
import numpy as np
from jax import lax
from jax.experimental import pallas as pl
from jax.experimental.pallas import tpu as pltpu
from jax.sharding import PartitionSpec as P

TAPS = 4
HISTORY = TAPS - 1
NCH = 256
C = 128
R = 128
FR = 16
NROW = 32
NTM = 8
RHERE = R // NROW
KHERE = NCH // NROW
RK = RHERE * KHERE
PARTS = 4
PART = NROW // PARTS
FAR = 5
VMEM_BYTES = 54656 * 1024
MESH_ID = pl.DeviceIdType.MESH


def pfb_window():
    points = np.arange(TAPS * NCH, dtype=np.float64)
    offset = (points + 0.5) / NCH - TAPS / 2.0
    taper = 0.5 - 0.5 * np.cos(2.0 * math.pi * (points + 0.5) / (TAPS * NCH))
    shaped = (np.sinc(offset) * taper).reshape(TAPS, NCH)
    return np.concatenate([shaped, shaped], axis=1).astype(np.float32)


def dft_table(length):
    indices = np.arange(length)
    angle = (indices[:, None] * indices[None, :] % length) * (2.0 * math.pi / length)
    cosine = np.cos(angle) / math.sqrt(length)
    sine = np.sin(angle) / math.sqrt(length)
    upper = np.stack([cosine, -sine], axis=1)
    bottom = np.stack([sine, cosine], axis=1)
    return np.stack([upper, bottom], axis=0).astype(np.float32).astype(ml_dtypes.bfloat16)


def tables():
    fine = dft_table(NCH).reshape(2 * NCH, 2, NROW, KHERE).transpose(2, 1, 3, 0)
    fine = fine.reshape(2 * NCH, 2 * NCH)
    column = dft_table(C).reshape(2 * C, 2 * C)
    row = dft_table(R).transpose(2, 3, 0, 1).reshape(2 * R, 2 * R)
    rest, parts = pfb_window(), []
    for _ in range(3):
        parts.append(rest.astype(ml_dtypes.bfloat16))
        rest = rest - parts[-1].astype(np.float32)
    assert not rest.any()
    parts.append(np.zeros_like(parts[0]))
    return np.concatenate([fine, np.concatenate([column, row], axis=1)] + parts, axis=0)


def kernel(
    volt_hbm, table_hbm, acc,
    volt, window, fine, beam, weighted, send, recv, mid,
    load_sem, table_sem, halo_sem, send_sem, recv_sem, go_sem,
):
    tm = lax.axis_index("tm")
    me = lax.axis_index("row")
    x, z, core = me // 16, (me // 2) % 8, me % 2
    after, before = (tm + 1) % NTM, (tm + NTM - 1) % NTM

    def plane(i):
        return (z + 4 + (i + 1) // 2 * (1 - i % 2 * 2)) % 8

    half_ring = NROW // 2

    def device(there, dx, dc):
        return (x if dx == 0 else 1 - x) * half_ring + 2 * there + (core if dc == 0 else 1 - core)

    SPOTS = ((1, 1), (1, 0), (0, 1), (0, 0))

    def load(g):
        return pltpu.make_async_copy(volt_hbm.at[g], volt.at[g + HISTORY], load_sem.at[g])

    def load_half(g, half):
        rows = pl.ds(half * 2 * C, 2 * C)
        return pltpu.make_async_copy(
            volt_hbm.at[g, rows], volt.at[g + HISTORY, rows], load_sem.at[g + FR * half]
        )

    window_copy, *fine_copies, beam_copy = [
        pltpu.make_async_copy(table_hbm.at[pl.ds(start, ref.shape[0])], ref, table_sem.at[i])
        for i, (start, ref) in enumerate(
            (
                (2 * NCH + 2 * C, window),
                (0, fine.at[pl.ds(0, NCH)]),
                (NCH, fine.at[pl.ds(NCH, NCH)]),
                (2 * NCH, beam),
            )
        )
    ]
    window_copy.start()
    for g in range(TAPS):
        load_half(g, 0).start()
    for copy in fine_copies:
        copy.start()

    barrier = pltpu.get_barrier_semaphore()
    near_ear, slab_ear = 2 * z + 1, NROW // 2 + 1
    is_near_ear, is_slab_ear = me == near_ear, me == slab_ear
    hears_all = jnp.logical_not(is_near_ear | is_slab_ear)
    mate_hears_all = (x == 1) & (z != 0)

    def signal(sem, **device_id):
        pl.semaphore_signal(sem, inc=1, device_id=device_id, device_id_type=MESH_ID)

    def tell_plane(sem, ear):
        chip = ear - 1
        signal(sem, row=chip)
        signal(sem, row=(chip + NROW // 2) % NROW)
        signal(sem, row=(ear + NROW // 2) % NROW)

    def greet(i, carry):
        there = plane(i)
        for side in range(2):
            signal(barrier, row=side * half_ring + 2 * there)

        @pl.when(there != 0)
        def _():
            signal(barrier, row=half_ring + 2 * there + 1)

        return carry

    for dz in (1, 7):
        signal(barrier, row=2 * ((z + dz) % 8) + 1)

    @pl.when(jnp.logical_not(is_near_ear))
    def _():
        signal(barrier, row=near_ear)

    @pl.when(core == 1)
    def _():
        signal(barrier, row=me - 1)

    @pl.when((z != 0) & (me != half_ring + 2 * z + 1))
    def _():
        signal(barrier, row=half_ring + 2 * z + 1)

    signal(barrier, row=(1 - x) * half_ring + 2 * z)
    lax.fori_loop(0, 7, greet, 0)

    for g in range(TAPS):
        load_half(g, 1).start()

    def load_more(g, carry):
        load(g).start()
        return carry

    lax.fori_loop(TAPS, FR, load_more, 0)
    beam_copy.start()

    halo = pltpu.make_async_remote_copy(
        src_ref=volt_hbm.at[pl.ds(FR - HISTORY, HISTORY)],
        dst_ref=volt.at[pl.ds(0, HISTORY)],
        send_sem=halo_sem.at[0],
        recv_sem=halo_sem.at[1],
        device_id={"tm": after},
        device_id_type=MESH_ID,
    )

    everything = pl.ds(0, RK)

    def half_of_block(half):
        return pl.ds(pl.multiple_of(half * (RK // 2), RK // 2), RK // 2)

    def spectrum(g, half, before_transform):
        parts = window[...].astype(jnp.float32)
        w = parts[:TAPS] + parts[TAPS : 2 * TAPS] + parts[2 * TAPS : 3 * TAPS]

        def chunk(i, carry):
            rows = pl.ds(pl.multiple_of(half * 2 * C + i * 16, 16), 16)
            total = w[0:1] * volt[g, rows, :].astype(jnp.float32)
            for tap in range(1, TAPS):
                total = total + w[tap : tap + 1] * volt[g + tap, rows, :].astype(jnp.float32)
            weighted[pl.ds(pl.multiple_of(i * 16, 16), 16), :] = total.astype(jnp.bfloat16)
            return carry

        lax.fori_loop(0, 2 * C // 16, chunk, 0, unroll=2)
        before_transform()
        out = lax.dot_general(
            fine[...],
            weighted[...],
            (((1,), (1,)), ((), ())),
            preferred_element_type=jnp.float32,
        ).reshape(NROW, 2, KHERE, 2 * C)
        for q in range(2):
            both = jnp.concatenate([out[:, q, :, :C], out[:, q, :, C:]], axis=1)
            send[g, :, half_of_block(half), q * C : (q + 1) * C] = both.astype(jnp.bfloat16)

    def dispatch(g, rows, start, end):
        def post(to):
            pltpu.make_async_remote_copy(
                src_ref=send.at[g, to, rows],
                dst_ref=recv.at[g, me, rows],
                send_sem=send_sem.at[g],
                recv_sem=recv_sem.at[g],
                device_id={"row": to},
                device_id_type=MESH_ID,
            ).start()

        def one(i, carry):
            there = plane(i)
            for dx, dc in SPOTS:
                post(device(there, dx, dc))
            return carry

        lax.fori_loop(start, min(end, 7), one, 0)
        if end == 8:
            for dx, dc in SPOTS[:3]:
                post(device(z, dx, dc))

    def keep(g):
        pltpu.make_async_copy(
            send.at[g, me], recv.at[g, me], recv_sem.at[g]
        ).start()

    def beams(g):
        pltpu.make_async_copy(send.at[g], recv.at[g], recv_sem.at[g]).wait()
        for part in range(PARTS):
            rows = R * KHERE // PARTS
            sources = pl.ds(part * PART, PART)
            block = recv[g, sources].reshape(rows, 2 * C)
            out = jnp.dot(block, beam[:, : 2 * C], preferred_element_type=jnp.float32)
            for q in range(2):
                mid[q, part * rows : (part + 1) * rows, :] = out[:, q * C : (q + 1) * C]
        for pair in range(KHERE // 2):
            sides = []
            for k in (2 * pair, 2 * pair + 1):
                parts = [mid[q, pl.ds(k, R, stride=KHERE), :] for q in range(2)]
                sides.append(jnp.concatenate(parts, axis=0).astype(jnp.bfloat16))
            field = jnp.dot(
                beam[:, 2 * C :], jnp.concatenate(sides, axis=1), preferred_element_type=jnp.float32
            )
            power = (field[:R] * field[:R] + field[R:] * field[R:]) * (1.0 / FR)
            for i in range(2):
                acc[2 * pair + i] += power[:, i * C : (i + 1) * C]

    def relay_near():
        @pl.when(is_near_ear)
        def _():
            pl.semaphore_wait(barrier, 3 + 2 * 4)
            tell_plane(go_sem.at[0], near_ear)

    def enter_near():
        @pl.when(jnp.logical_not(is_near_ear))
        def _():
            pl.semaphore_wait(go_sem.at[0], 1)

    def enter():
        @pl.when(hears_all)
        def _():
            pl.semaphore_wait(barrier, NROW - 1)

        @pl.when((core == 0) & jnp.logical_not(mate_hears_all))
        def _():
            signal(go_sem.at[1], row=me + 1)

        @pl.when(jnp.logical_not(hears_all))
        def _():
            pl.semaphore_wait(go_sem.at[1], 1)

        @pl.when(is_slab_ear)
        def _():
            signal(barrier, tm=before)

    def meet_next_slab():
        @pl.when(is_slab_ear)
        def _():
            pl.semaphore_wait(barrier, 1)

            def tell(i, carry):
                for dx, dc in SPOTS:
                    signal(go_sem.at[2], row=device(plane(i), dx, dc))
                return carry

            lax.fori_loop(0, 7, tell, 0)
            for dx, dc in SPOTS[:3]:
                signal(go_sem.at[2], row=device(z, dx, dc))

        @pl.when(jnp.logical_not(is_slab_ear))
        def _():
            pl.semaphore_wait(go_sem.at[2], 1)

    acc[...] = jnp.zeros_like(acc)

    def produce(n, carry):
        g, half = (n // 2 + HISTORY) % FR, n % 2

        @pl.when(n == 0)
        def _():
            window_copy.wait()
            for i in range(TAPS):
                load_half(i, 0).wait()
            relay_near()

        @pl.when(n == 1)
        def _():
            for i in range(TAPS):
                load_half(i, 1).wait()

        @pl.when((n > 1) & (half == 0) & (g >= TAPS))
        def _():
            load(g).wait()

        @pl.when(n == 2 * (FR - HISTORY))
        def _():
            halo.wait()

        def fine_ready():
            @pl.when(n == 0)
            def _():
                for copy in fine_copies:
                    copy.wait()

        spectrum(g, half, fine_ready)

        @pl.when(n == 0)
        def _():
            enter_near()

        @pl.when(n < 4)
        def _():
            dispatch(g, half_of_block(half), FAR, 8)

        @pl.when(n == 3)
        def _():
            enter()

            def rest(f, carry):
                dispatch(f, everything, 0, FAR)
                keep(f)
                return carry

            lax.fori_loop(HISTORY, HISTORY + 2, rest, 0)

        @pl.when((n > 3) & (half == 1))
        def _():
            dispatch(g, everything, 0, 8)
            keep(g)

        @pl.when(n == 7)
        def _():
            meet_next_slab()
            halo.start()

        return carry

    lax.fori_loop(0, 2 * FR, produce, 0)
    beam_copy.wait()

    def sent(g):
        some = pl.ds(0, NROW - 1)
        pltpu.make_async_copy(send.at[g, some], recv.at[g, some], send_sem.at[g]).wait()

    def gather(i, carry):
        beams((i + HISTORY) % FR)

        @pl.when(i < FR - 1)
        def _():
            sent((i + HISTORY) % FR)

        return carry

    lax.fori_loop(0, FR, gather, 0)
    sent(HISTORY - 1)


def body(voltage):
    frames, rows, columns, width = voltage.shape
    in_hbm = pl.BlockSpec(memory_space=pltpu.HBM)
    power = pl.pallas_call(
        kernel,
        out_shape=jax.ShapeDtypeStruct((KHERE, R, C), jnp.float32),
        in_specs=[in_hbm] * 2,
        out_specs=pl.BlockSpec(memory_space=pltpu.VMEM),
        scratch_shapes=[
            pltpu.VMEM((FR + HISTORY, RHERE * C, 2 * NCH), jnp.bfloat16),
            pltpu.VMEM((4 * TAPS, 2 * NCH), jnp.bfloat16),
            pltpu.VMEM((2 * NCH, 2 * NCH), jnp.bfloat16),
            pltpu.VMEM((2 * C, 4 * C), jnp.bfloat16),
            pltpu.VMEM((RHERE * C // 2, 2 * NCH), jnp.bfloat16),
            pltpu.VMEM((FR, NROW, RK, 2 * C), jnp.bfloat16),
            pltpu.VMEM((FR, NROW, RK, 2 * C), jnp.bfloat16),
            pltpu.VMEM((2, R * KHERE, C), jnp.float32),
            pltpu.SemaphoreType.DMA((FR + HISTORY + 1,)),
            pltpu.SemaphoreType.DMA((4,)),
            pltpu.SemaphoreType.DMA((2,)),
            pltpu.SemaphoreType.DMA((FR,)),
            pltpu.SemaphoreType.DMA((FR,)),
            pltpu.SemaphoreType.REGULAR((3,)),
        ],
        compiler_params=pltpu.CompilerParams(
            collective_id=0, has_side_effects=True, vmem_limit_bytes=VMEM_BYTES
        ),
        name="beamformer",
    )(
        voltage.reshape(frames, rows * columns, width),
        jnp.asarray(tables()),
    )
    return power[None]


def solution(mesh):
    return jax.shard_map(
        body,
        mesh=mesh,
        in_specs=(P("tm", "row", None, None),),
        out_specs=P("tm", "row", None, None),
        check_vma=False,
    )
```
